256 devices in a mesh: pair: 128 (over z, y, x), blk: 2 (over core).
Axes of the slice: x: 4, y: 4, z: 8, core: 2. Of those that a mesh axis runs over, the one named last changes fastest.
Arguments:
- amplitudes: float32 [128, 1024, 1024], P('pair', 'blk'), may hold values from -6 to 6
- domain_mask: int32 [128, 16, 16], P('pair', 'blk'), may hold values 0 or 1
- integrals: float32 [2, 1024, 1024], P(None, 'blk'), may hold values from -0.125 to 0.125
Outputs:
- residual: float32 [64, 1024, 1024], P(None, ('blk', 'pair'))
The draws below stay inside these ranges and needn't reach their ends.
All inputs are finite; a program needn't handle non-finite values. No bound on the sum of `domain_mask` on one device may be relied on, other than what follows from the above.
Results may differ from the reference program's by a relative error of at most 0.00007.
Values sent between devices are 32-bit elements; how exact they have to be, the bound alone decides.
No kernel may reach another device: no remote copies, remote signals or barrier semaphores. Data moves between devices by JAX's collectives and lax.ppermute only.
A program may use at most 64 MiB of HBM per device.

```python
import jax
import jax.numpy as jnp
from jax import lax

V = 1024
VB = 1024
TILE = 64
NK = 2
P_SIZE = 128
NI = 64


def set_ends(drawn, key, least, high):
    longest = drawn.shape.index(max(drawn.shape))
    spots = []
    for shift in (0, 1):
        where = [jax.random.randint(jax.random.fold_in(key, axis), (), 0, length) for axis, length in enumerate(drawn.shape)]
        where[longest] = (where[longest] + shift) % drawn.shape[longest]
        spots.append(tuple(where))
    return drawn.at[spots[0]].set(least).at[spots[1]].set(high)


def level_of(stream_key, dims, split, smallest, high):
    def one(position, parts):
        heights = jax.random.uniform(jax.random.fold_in(jax.random.fold_in(stream_key, 6), position), (parts,), jnp.float32, smallest / len(split), high / len(split))
        return jnp.repeat(jnp.exp(heights), dims[position] // parts).reshape((-1,) + (1,) * (len(dims) - position - 1))

    factor_of = one(*split[0])
    for cut in split[1:]:
        factor_of = factor_of * one(*cut)
    return factor_of


def normal_values(own_key, extent, width, reach, shards=(), held_as=jnp.bfloat16):
    factor_of = level_of(own_key, extent, shards, -0.22, 0.18) if shards else 1.0
    array = jax.random.normal(own_key, extent, jnp.float32) * width * factor_of
    return jnp.minimum(jnp.maximum(array, -reach), reach).astype(held_as)


def setup_inputs(seed: int = 0) -> dict:
    splits = jax.random.split(jax.random.key(seed), 4)
    amplitudes = normal_values(splits[0], (P_SIZE, V, V), 1.0, 6.0, ((0, 128), (1, 2)), jnp.float32)
    domain_mask = set_ends((jax.random.randint(splits[1], (P_SIZE, V // TILE, V // TILE), 0, 2) < 1).astype(jnp.int32), jax.random.fold_in(splits[1], 1), 0, 1)
    integrals = normal_values(splits[2], (NK, V, VB), (NK * V) ** -0.5, 0.125, ((1, 2),), jnp.float32)
    return dict(amplitudes=amplitudes, domain_mask=domain_mask, integrals=integrals)


def reference(amplitudes, domain_mask, integrals):
    tiles = V // TILE
    expanded = domain_mask.astype(amplitudes.dtype)[:, :, None, :, None]
    masked = (amplitudes.reshape(P_SIZE, tiles, TILE, tiles, TILE) * expanded).reshape(NI, NK, V, V)
    return jnp.einsum("ikac,kcb->iab", masked, integrals, precision=lax.Precision.HIGHEST)
```

```python
import functools
import jax
import jax.numpy as jnp
from jax import lax
from jax.experimental import pallas as pl
from jax.experimental.pallas import tpu as pltpu
from jax.sharding import PartitionSpec as P

TILE = 64
LANES = 128
X = 4
R = 4
PIECES = 4


def vmem():
    return pl.BlockSpec(memory_space=pltpu.VMEM)


def smem():
    return pl.BlockSpec(memory_space=pltpu.SMEM)


def hbm():
    return pl.BlockSpec(memory_space=pltpu.HBM)


def split(value):
    high = value.astype(jnp.bfloat16)
    low = (value - high.astype(jnp.float32)).astype(jnp.bfloat16)
    return high, low


def dot(a, b):
    return jnp.dot(a, b, preferred_element_type=jnp.float32)


def product(a_high, a_low, b_high, b_low):
    return dot(a_high, b_high) + (dot(a_high, b_low) + dot(a_low, b_high))


def prepare_kernel(where_ref, t_ref, mask_ref, send_ref, own_ref, held_ref, mask_held, sems):
    rows, width = t_ref.shape[1:]
    tiles_a, tiles_c = mask_ref.shape[1:]
    groups = rows // (X * R)
    tiles = width // LANES
    mask_copy = pltpu.make_async_copy(mask_ref.at[0], mask_held, sems.at[tiles])
    mask_copy.start()
    copies = []
    for t in range(tiles):
        copy = pltpu.make_async_copy(t_ref.at[0, :, pl.ds(t * LANES, LANES)], held_ref.at[t], sems.at[t])
        copy.start()
        copies.append(copy)
    per_tile = groups // tiles_a
    pick = (
        lax.broadcasted_iota(jnp.int32, (groups, tiles_a), 0) // per_tile
        == lax.broadcasted_iota(jnp.int32, (groups, tiles_a), 1)
    ).astype(jnp.float32)
    spread = (
        lax.broadcasted_iota(jnp.int32, (tiles_c, width), 1) // TILE
        == lax.broadcasted_iota(jnp.int32, (tiles_c, width), 0)
    ).astype(jnp.float32)
    mask_copy.wait()
    mask = dot(dot(pick, mask_held[...].astype(jnp.float32)), spread)
    outer = where_ref[0] == 1
    for t in range(tiles):
        copies[t].wait()
        cols = pl.ds(t * LANES, LANES)
        m = mask[:, t * LANES : (t + 1) * LANES]
        for h in range(2):
            x_outer, x_inner = (0, 1) if h == 0 else (3, 2)
            x_own = jnp.where(outer, x_outer, x_inner)
            x_send = jnp.where(outer, x_inner, x_outer)
            for r in range(R):
                at = pl.ds((r * 2 + h) * groups, groups)
                own_ref[at, cols] = held_ref[t, pl.ds(x_own * R + r, groups, X * R), :] * m
                send_ref[at, cols] = held_ref[t, pl.ds(x_send * R + r, groups, X * R), :] * m


def near_kernel(where_ref, own_ref, send_ref, w_ref, *refs):
    part_kernel(where_ref, own_ref, send_ref, w_ref, None, None, *refs)


def part_kernel(where_ref, own_ref, send_ref, w_ref, own_first, send_first, *refs):
    own_part, send_part, high_ref, low_ref, held_ref, sems = refs
    k, half, blk = where_ref[1], where_ref[2], where_ref[3]
    depth = w_ref.shape[1]
    piece = depth // PIECES

    def copies(which, of):
        return [
            pltpu.make_async_copy(
                w_ref.at[of, pl.ds(q * piece, piece)],
                held_ref.at[which, pl.ds(q * piece, piece)],
                sems.at[which, q],
            )
            for q in range(PIECES)
        ]

    mine = copies(0, k)
    for copy in mine:
        copy.start()

    @pl.when(blk == 0)
    def _():
        for copy in copies(1, 1 - k):
            copy.start()

    for copy in mine:
        copy.wait()
    cols = pl.ds(pl.multiple_of(half * depth, depth), depth)
    w_high, w_low = split(held_ref[0])

    def add(x_ref, first_ref, to_ref):
        x_high, x_low = split(x_ref[:, cols])
        term = product(x_high, x_low, w_high, w_low)
        to_ref[...] = term if first_ref is None else first_ref[...] + term

    @pl.when(blk == 1)
    def _():
        add(send_ref, send_first, send_part)

    add(own_ref, own_first, own_part)

    @pl.when(blk == 0)
    def _():
        for copy in copies(1, 1 - k):
            copy.wait()
        o_high, o_low = split(held_ref[1])
        high_ref[...] = o_high
        low_ref[...] = o_low


def place(out_ref, total):
    rows, width = total.shape
    groups = rows // (2 * R)
    tiles = width // LANES
    per = R * tiles
    for r in range(R):
        for h in range(2):
            row = (r * 2 + h) * groups
            for t in range(tiles):
                out_ref[pl.ds(h * per + t * R + r, groups, 2 * per), :] = total[
                    row : row + groups, t * LANES : (t + 1) * LANES
                ]


def last_kernel(where_ref, rows_ref, sums_ref, high0_ref, low0_ref, high1_ref, low1_ref, part_ref, out_ref):
    half, blk = where_ref[2], where_ref[3]
    depth = high0_ref.shape[0]

    @pl.when(blk == 0)
    def _():
        total = part_ref[...]
        for at, high, low in ((half, high0_ref, low0_ref), (1 - half, high1_ref, low1_ref)):
            cols = pl.ds(pl.multiple_of(at * depth, depth), depth)
            a_high, a_low = split(rows_ref[:, cols])
            total = total + product(a_high, a_low, high[...], low[...])
        place(out_ref, total)

    @pl.when(blk == 1)
    def _():
        place(out_ref, sums_ref[...] + part_ref[...])


def call(kernel, name, out_shape, in_specs, scratch=()):
    return pl.pallas_call(
        kernel,
        out_shape=out_shape,
        in_specs=in_specs,
        out_specs=jax.tree.map(lambda _: vmem(), out_shape),
        scratch_shapes=list(scratch),
        compiler_params=pltpu.CompilerParams(vmem_limit_bytes=32 * 2**20),
        cost_estimate=pl.CostEstimate(flops=1000, bytes_accessed=1000, transcendentals=0),
        name=name,
    )


def on_device(n_pair, halves, amplitudes, domain_mask, integrals):
    f32, bf16 = jnp.float32, jnp.bfloat16

    def of(*shape, dtype=f32):
        return jax.ShapeDtypeStruct(shape, dtype)

    rows, width = amplitudes.shape[1:]
    depth, columns = integrals.shape[1:]
    kept = rows // 2
    dests = kept // R
    tiles = columns // LANES
    x = lax.axis_index("pair") % X
    blk = lax.axis_index("blk")
    outer = ((x == 0) | (x == 3)).astype(jnp.int32)
    where = jnp.stack([outer, x % 2, blk, blk]).astype(jnp.int32)
    where_other = jnp.stack([outer, x % 2, 1 - blk, blk]).astype(jnp.int32)
    swaps = [[(2 * p + core, 2 * (p ^ 1) + core) for p in range(n_pair)] for core in range(2)]

    other = lax.ppermute(integrals, "blk", [(0, 1), (1, 0)])
    send, own = call(
        prepare_kernel,
        "prepare",
        [of(kept, width)] * 2,
        [smem(), hbm(), hbm()],
        [
            pltpu.VMEM((width // LANES, rows, LANES), f32),
            pltpu.VMEM(domain_mask.shape[1:], jnp.int32),
            pltpu.SemaphoreType.DMA((width // LANES + 1,)),
        ],
    )(where, amplitudes, domain_mask)
    got_rows = lax.ppermute(send, ("pair", "blk"), swaps[0])

    outs = [of(kept, columns)] * 2 + [of(depth, columns, dtype=bf16)] * 2
    scratch = [pltpu.VMEM((2, depth, columns), f32), pltpu.SemaphoreType.DMA((2, PIECES))]
    own_part, send_part, high0, low0 = call(
        near_kernel, "near", outs, [smem(), vmem(), vmem(), hbm()], scratch
    )(where, own, send, integrals)
    own_part, send_part, high1, low1 = call(
        part_kernel, "far", outs, [smem(), vmem(), vmem(), hbm(), vmem(), vmem()], scratch
    )(where_other, own, send, other, own_part, send_part)
    got_sums = lax.ppermute(send_part, ("pair", "blk"), swaps[1])
    block = call(last_kernel, "last", of(dests * R * tiles, LANES), [smem()] + [vmem()] * 7)(
        where, got_rows, got_sums, high0, low0, high1, low1, own_part
    )
    back = lax.all_to_all(
        block.reshape(dests, R * tiles, LANES),
        "pair",
        split_axis=0,
        concat_axis=0,
        tiled=True,
        axis_index_groups=halves,
    )
    return back.reshape(dests, tiles, R, LANES).transpose(0, 2, 1, 3).reshape(dests, R, columns)


def solution(mesh):
    n_pair = mesh.shape["pair"]
    halves = [
        [p for p in range(n_pair) if p % X in (0, 3)],
        [p for p in range(n_pair) if p % X in (1, 2)],
    ]
    return jax.shard_map(
        functools.partial(on_device, n_pair, halves),
        mesh=mesh,
        in_specs=(P("pair", "blk", None), P("pair", "blk", None), P(None, "blk", None)),
        out_specs=P(None, ("blk", "pair"), None),
        check_vma=False,
    )
```

```python
import functools
import jax
import jax.numpy as jnp
from jax import lax
from jax.experimental import pallas as pl
from jax.experimental.pallas import tpu as pltpu
from jax.sharding import PartitionSpec as P

TILE = 64
LANES = 128
X = 4
Y = 4
Z = 8
R = 4
FIRST = (0, 2)
SECOND = (1, 3)
PIECES = 4
PIECE = 2 * R * Z
ADD_FLOPS = 10**11


def vmem():
    return pl.BlockSpec(memory_space=pltpu.VMEM)


def hbm():
    return pl.BlockSpec(memory_space=pltpu.HBM)


def in_hbm(value):
    return pltpu.with_memory_space_constraint(value, pltpu.HBM)


def here():
    me = lax.axis_index("pair")
    return lax.rem(me, X), lax.rem(lax.div(me, X), Y), lax.axis_index("blk")


def split(value):
    high = value.astype(jnp.bfloat16)
    low = (value - high.astype(jnp.float32)).astype(jnp.bfloat16)
    return high, low


def dot(a, b):
    return jnp.dot(a, b, preferred_element_type=jnp.float32)


def product(a_high, a_low, b_high, b_low):
    return dot(a_high, b_high) + (dot(a_high, b_low) + dot(a_low, b_high))


def tile_rows(mask_ref, shift, width):
    tiles = mask_ref.shape[1]
    column = lax.div(lax.broadcasted_iota(jnp.int32, (tiles, width), 1), TILE)
    spread = lax.rem(column + shift, tiles) == lax.broadcasted_iota(jnp.int32, (tiles, width), 0)
    return dot(mask_ref[...].astype(jnp.float32), spread.astype(jnp.float32))


def first_kernel(t_ref, mask_ref, near_ref, far_ref, held_ref, mask_held, sems):
    width = t_ref.shape[3]
    tiles = width // LANES
    x, y, blk = here()
    outer = (x == 0) | (x == X - 1)
    mask_copy = pltpu.make_async_copy(mask_ref.at[0], mask_held, sems.at[len(FIRST) * tiles])
    mask_copy.start()
    copies = []
    for t in range(tiles):
        lanes = pl.multiple_of(lax.rem(t + blk * (tiles // 2), tiles) * LANES, LANES)
        for j, dy in enumerate(FIRST):
            copy = pltpu.make_async_copy(
                t_ref.at[:, lax.rem(y + dy, Y), :, pl.ds(lanes, LANES)],
                held_ref.at[t, j],
                sems.at[t * len(FIRST) + j],
            )
            copy.start()
            copies.append(copy)
    mask_copy.wait()
    mask = tile_rows(mask_held, blk * (mask_ref.shape[2] // 2), width)
    for t in range(tiles):
        out_ref = near_ref if t < tiles // 2 else far_ref
        cols = pl.ds(t % (tiles // 2) * LANES, LANES)
        m = mask[:, t * LANES : (t + 1) * LANES]
        for j in range(len(FIRST)):
            copies[t * len(FIRST) + j].wait()
            rows = held_ref.at[t, j].reshape(Z * X * R, LANES)
            for r in range(R):
                for h in range(2):
                    x_outer, x_inner = (0, 1) if h == 0 else (3, 2)
                    a = rows[pl.ds(x_outer * R + r, Z, X * R), :]
                    b = rows[pl.ds(x_inner * R + r, Z, X * R), :]
                    out_ref[pl.ds(((j * R + r) * 2 + h) * Z, Z), cols] = jnp.where(outer, b, a) * m


def rest_kernel(t_ref, mask_ref, after_ref, rest_ref, held_ref, mask_held, sems):
    del after_ref
    rows, width = t_ref.shape[1:]
    part = rows // 4
    x, y, blk = here()
    outer = (x == 0) | (x == X - 1)
    plane = X * Y * R
    tiles = width // LANES
    mask_copy = pltpu.make_async_copy(mask_ref.at[0], mask_held, sems.at[tiles])
    mask_copy.start()
    copies = []
    for t in range(tiles):
        copy = pltpu.make_async_copy(t_ref.at[0, :, pl.ds(t * LANES, LANES)], held_ref.at[t], sems.at[t])
        copy.start()
        copies.append(copy)
    mask_copy.wait()
    mask = tile_rows(mask_held, 0, width)
    for t in range(tiles):
        copies[t].wait()
        cols = pl.ds(t * LANES, LANES)
        m = mask[:, t * LANES : (t + 1) * LANES]
        for c, chunk in enumerate((FIRST, SECOND)):
            for j, dy in enumerate(chunk):
                at_y = lax.rem(y + dy, Y) * (X * R)
                for r in range(R):
                    for h in range(2):
                        x_outer, x_inner = (0, 1) if h == 0 else (3, 2)
                        a = held_ref[t, pl.ds(at_y + (x_outer * R + r), Z, plane), :] * m
                        b = held_ref[t, pl.ds(at_y + (x_inner * R + r), Z, plane), :] * m
                        at = ((j * R + r) * 2 + h) * Z
                        rest_ref[pl.ds(c * part + at, Z), cols] = jnp.where(outer, a, b)
                        if c:
                            rest_ref[pl.ds(2 * part + at, Z), cols] = jnp.where(outer, b, a)


def own_kernel(has_first, x_ref, w_ref, *refs):
    x, _, blk = here()
    k = lax.rem(x, 2)
    half = 1 - blk if has_first else blk
    first_ref = refs[0] if has_first else None
    *part_refs, high_ref, low_ref, held_ref, sems = refs[has_first:]
    depth = w_ref.shape[1]
    piece = depth // PIECES
    copies = []
    for which, of in enumerate((k, 1 - k)):
        for q in range(PIECES):
            copy = pltpu.make_async_copy(
                w_ref.at[of, pl.ds(q * piece, piece)],
                held_ref.at[which, pl.ds(q * piece, piece)],
                sems.at[which, q],
            )
            copy.start()
            copies.append(copy)
    cols = pl.ds(pl.multiple_of(half * depth, depth), depth)
    x_high, x_low = split(x_ref[:, cols])
    total = first_ref[...] if has_first else None
    for copy in copies[:PIECES]:
        copy.wait()
    w_high, w_low = split(held_ref[0])
    term = product(x_high, x_low, w_high, w_low)
    total = term if total is None else total + term
    base = 0
    for part_ref in part_refs:
        count = part_ref.shape[0]
        part_ref[...] = total[base : base + count]
        base += count
    for copy in copies[PIECES:]:
        copy.wait()
    o_high, o_low = split(held_ref[1])
    high_ref[...] = o_high
    low_ref[...] = o_low


def near_kernel(got_ref, high_ref, low_ref, part_ref, out_ref):
    out_ref[...] = part_ref[...] + product(*split(got_ref[...]), high_ref[...], low_ref[...])


def last_kernel(got_ref, high_ref, low_ref, part_ref, out_ref):
    total = part_ref[...] + product(*split(got_ref[...]), high_ref[...], low_ref[...])
    n, tiles = len(FIRST), total.shape[1] // LANES
    for j in range(n):
        put(out_ref, total[j * PIECE : (j + 1) * PIECE], j * R * tiles, n * R * tiles)


def put(out_ref, total, start, block):
    tiles = total.shape[1] // LANES
    for r in range(R):
        for h in range(2):
            row = (r * 2 + h) * Z
            for t in range(tiles):
                out_ref[pl.ds(h * block + start + t * R + r, Z, 2 * block), :] = total[
                    row : row + Z, t * LANES : (t + 1) * LANES
                ]


def add_kernel(got_ref, part_ref, *out_refs):
    tiles = got_ref.shape[1] // LANES
    for j, out_ref in enumerate(out_refs):
        rows = pl.ds(j * PIECE, PIECE)
        put(out_ref, got_ref[rows, :] + part_ref[rows, :], 0, R * tiles)


def turn_kernel(in_ref, out_ref):
    block = out_ref.shape[0] // (2 * Z)
    for n in range(2 * Z):
        out_ref[pl.ds(n * block, block), :] = in_ref[pl.ds((n * len(FIRST) + 1) * block, block), :]


def gather_kernel(*refs):
    *in_refs, out_ref = refs
    block = in_refs[0].shape[0] // (2 * Z)
    for j, in_ref in enumerate(in_refs):
        for n in range(2 * Z):
            out_ref[pl.ds((n * len(in_refs) + j) * block, block), :] = in_ref[pl.ds(n * block, block), :]


def merge_kernel(first_ref, moved_ref, second_ref, out_ref):
    block = out_ref.shape[0] // (2 * Y * Z)
    _, here_y, _ = here()
    for dy in range(Y):
        y = lax.rem(here_y - dy + Y, Y)
        for n in range(2 * Z):
            if dy == FIRST[1]:
                value = moved_ref[pl.ds(n * block, block), :]
            elif dy == FIRST[0]:
                value = first_ref[pl.ds(n * len(FIRST) * block, block), :]
            else:
                value = second_ref[pl.ds((n * len(SECOND) + SECOND.index(dy)) * block, block), :]
            z, h = n // 2, n % 2
            out_ref[pl.ds(pl.multiple_of(((z * Y + y) * 2 + h) * block, block), block), :] = value


def call(kernel, name, out_shape, in_specs, scratch=(), flops=1000):
    return pl.pallas_call(
        kernel,
        out_shape=out_shape,
        in_specs=in_specs,
        out_specs=jax.tree.map(lambda _: vmem(), out_shape),
        scratch_shapes=list(scratch),
        compiler_params=pltpu.CompilerParams(vmem_limit_bytes=24 * 2**20),
        cost_estimate=pl.CostEstimate(flops=flops, bytes_accessed=1000, transcendentals=0),
        name=name,
    )


def on_device(n_pair, groups, amplitudes, domain_mask, integrals):
    f32, bf16 = jnp.float32, jnp.bfloat16

    def of(*shape, dtype=f32):
        return jax.ShapeDtypeStruct(shape, dtype)

    rows, width = amplitudes.shape[1:]
    depth, columns = integrals.shape[1:]
    kept = rows // 2
    dests = kept // R
    tiles = columns // LANES
    swap = [(p, p ^ 1) for p in range(n_pair)]
    other = lax.ppermute(integrals, "blk", [(0, 1), (1, 0)])
    n_tiles = width // LANES
    mask_scratch = pltpu.VMEM(domain_mask.shape[1:], jnp.int32)
    send_near, send_far = call(
        first_kernel,
        "first",
        [of(2 * PIECE, width // 2)] * 2,
        [hbm(), hbm()],
        [
            pltpu.VMEM((n_tiles, len(FIRST), Z, X * R, LANES), f32),
            mask_scratch,
            pltpu.SemaphoreType.DMA((len(FIRST) * n_tiles + 1,)),
        ],
    )(in_hbm(amplitudes.reshape(Z, Y, X * R, width)), in_hbm(domain_mask))
    got_near = lax.ppermute(send_near, "pair", swap)
    got_far = lax.ppermute(send_far, "pair", swap)
    rest = call(
        rest_kernel,
        "rest",
        of(6 * PIECE, width),
        [hbm(), hbm(), pl.BlockSpec(memory_space=pl.ANY)],
        [pltpu.VMEM((n_tiles, rows, LANES), f32), mask_scratch, pltpu.SemaphoreType.DMA((n_tiles + 1,))],
    )(in_hbm(amplitudes), in_hbm(domain_mask), send_far)

    halves_w = [of(depth, columns, dtype=bf16)] * 2
    scratch = [pltpu.VMEM((2, depth, columns), f32), pltpu.SemaphoreType.DMA((2, PIECES))]
    part, high0, low0 = call(
        functools.partial(own_kernel, False),
        "own_near",
        [of(6 * PIECE, columns)] + halves_w,
        [vmem(), hbm()],
        scratch,
    )(rest, in_hbm(integrals))
    part0, part1, send1, high1, low1 = call(
        functools.partial(own_kernel, True),
        "own_far",
        [of(2 * PIECE, columns)] * 3 + halves_w,
        [vmem(), hbm(), vmem()],
        scratch,
    )(rest, other, part)
    send1, got_near, got_far = lax.optimization_barrier((send1, got_near, got_far))
    got1 = lax.ppermute(send1, "pair", swap)

    def along_y(value, dy):
        perm = []
        for p in range(n_pair):
            pz, py, px = p // (X * Y), p // X % Y, p % X
            perm.append((p, (pz * Y + (py + dy) % Y) * X + px))
        return lax.ppermute(value, "pair", perm)

    def across(block):
        out = lax.all_to_all(
            block.reshape(2 * Z, -1, LANES),
            "pair",
            split_axis=0,
            concat_axis=0,
            tiled=True,
            axis_index_groups=groups,
        )
        return out.reshape(-1, LANES)

    half, piece = of(2 * PIECE * tiles, LANES), of(PIECE * tiles, LANES)
    part0 = call(near_kernel, "near", of(2 * PIECE, columns), [vmem()] * 4)(got_near, high0, low0, part0)
    block0 = call(last_kernel, "last", half, [vmem()] * 4)(got_far, high1, low1, part0)
    back0 = across(block0)
    pieces = call(add_kernel, "add", [piece] * 2, [vmem()] * 2, (), ADD_FLOPS)(got1, part1)
    pieces = [along_y(value, dy) for value, dy in zip(pieces, SECOND)]
    block1 = call(gather_kernel, "gather", half, [vmem()] * 2)(*pieces)
    back1 = across(block1)
    moved = along_y(call(turn_kernel, "turn", piece, [vmem()])(back0), FIRST[1])
    whole = call(merge_kernel, "merge", of(4 * PIECE * tiles, LANES), [vmem()] * 3)(back0, moved, back1)
    return whole.reshape(dests, tiles, R, LANES).transpose(0, 2, 1, 3).reshape(dests, R, columns)


def solution(mesh):
    n_pair = mesh.shape["pair"]
    groups = [
        [(z * Y + y) * X + x for z in range(Z) for x in pair] for y in range(Y) for pair in ((0, 3), (1, 2))
    ]
    return jax.shard_map(
        functools.partial(on_device, n_pair, groups),
        mesh=mesh,
        in_specs=(P("pair", "blk", None), P("pair", "blk", None), P(None, "blk", None)),
        out_specs=P(None, ("blk", "pair"), None),
        check_vma=False,
    )
```

```python
import functools
import jax
import jax.numpy as jnp
from jax import lax
from jax.experimental import pallas as pl
from jax.experimental.pallas import tpu as pltpu
from jax.sharding import PartitionSpec as P

TILE = 64
LANES = 128
X = 4
Y = 4
Z = 8
R = 4
FIRST = 2
MOVED = (1, 3)
SECOND = MOVED + (0,)
PARTS = 4
PIECE = 2 * R * Z
ADD_FLOPS = 10**11
START_Z = 5


def vmem():
    return pl.BlockSpec(memory_space=pltpu.VMEM)


def hbm():
    return pl.BlockSpec(memory_space=pltpu.HBM)


def in_hbm(value):
    return pltpu.with_memory_space_constraint(value, pltpu.HBM)


def here():
    me = lax.axis_index("pair")
    return lax.rem(me, X), lax.rem(lax.div(me, X), Y), lax.axis_index("blk")


def split(value):
    high = value.astype(jnp.bfloat16)
    low = (value - high.astype(jnp.float32)).astype(jnp.bfloat16)
    return high, low


def dot(a, b):
    return jnp.dot(a, b, preferred_element_type=jnp.float32)


def product(a_high, a_low, b_high, b_low):
    return dot(a_high, b_high) + (dot(a_high, b_low) + dot(a_low, b_high))


def tile_rows(mask_ref, shift, width):
    tiles = mask_ref.shape[1]
    column = lax.div(lax.broadcasted_iota(jnp.int32, (tiles, width), 1), TILE)
    spread = lax.rem(column + shift, tiles) == lax.broadcasted_iota(jnp.int32, (tiles, width), 0)
    return dot(mask_ref[...].astype(jnp.float32), spread.astype(jnp.float32))


def first_kernel(t_ref, mask_ref, out_ref, held_ref, mask_held, sems):
    width = t_ref.shape[3]
    tiles = width // LANES
    x, y, blk = here()
    partner = x + 1 - 2 * lax.rem(x, 2)
    mask_copy = pltpu.make_async_copy(mask_ref.at[0], mask_held, sems.at[tiles])
    mask_copy.start()
    copies = []
    for t in range(tiles):
        lanes = pl.multiple_of(lax.rem(t + blk * (tiles // 2), tiles) * LANES, LANES)
        copy = pltpu.make_async_copy(
            t_ref.at[:, lax.rem(y + FIRST, Y), :, pl.ds(lanes, LANES)], held_ref.at[t], sems.at[t]
        )
        copy.start()
        copies.append(copy)
    mask_copy.wait()
    mask = tile_rows(mask_held, blk * (mask_ref.shape[2] // 2), width)
    for t in range(tiles):
        cols = pl.ds(t * LANES, LANES)
        m = mask[:, t * LANES : (t + 1) * LANES]
        copies[t].wait()
        rows = held_ref.at[t].reshape(Z * X * R, LANES)
        for r in range(R):
            for h in range(2):
                value = rows[pl.ds(end(partner, h) * R + r, Z, X * R), :]
                out_ref[pl.ds((r * 2 + h) * Z, Z), cols] = value * m


def end(x, h):
    outer = (x == 0) | (x == X - 1)
    return jnp.where(outer, h * (X - 1), 1 + h)


def rest_kernel(t_ref, mask_ref, after_ref, rest_ref, held_ref, mask_held, sems):
    del after_ref
    rows, width = t_ref.shape[1:]
    x, y, blk = here()
    partner = x + 1 - 2 * lax.rem(x, 2)
    plane = X * Y * R
    tiles = width // LANES
    mask_copy = pltpu.make_async_copy(mask_ref.at[0], mask_held, sems.at[tiles])
    mask_copy.start()
    copies = []
    for t in range(tiles):
        copy = pltpu.make_async_copy(t_ref.at[0, :, pl.ds(t * LANES, LANES)], held_ref.at[t], sems.at[t])
        copy.start()
        copies.append(copy)
    mask_copy.wait()
    mask = tile_rows(mask_held, 0, width)
    wanted = [(dy, x) for dy in (FIRST,) + SECOND] + [(dy, partner) for dy in SECOND]
    for t in range(tiles):
        copies[t].wait()
        cols = pl.ds(t * LANES, LANES)
        m = mask[:, t * LANES : (t + 1) * LANES]
        for n, (dy, device) in enumerate(wanted):
            for h in range(2):
                base = (lax.rem(y + dy, Y) * X + end(device, h)) * R
                for r in range(R):
                    value = held_ref[t, pl.ds(base + r, Z, plane), :]
                    rest_ref[pl.ds(n * PIECE + (r * 2 + h) * Z, Z), cols] = value * m


def own_kernel(has_first, x_ref, w_ref, *refs):
    x, _, blk = here()
    k = lax.rem(x, 2)
    half = 1 - blk if has_first else blk
    first_ref = refs[0] if has_first else None
    *part_refs, high_ref, low_ref, held_ref, sems = refs[has_first:]
    depth = w_ref.shape[1]
    piece = depth // PARTS
    copies = []
    for which, of in enumerate((k, 1 - k)):
        for q in range(PARTS):
            copy = pltpu.make_async_copy(
                w_ref.at[of, pl.ds(q * piece, piece)],
                held_ref.at[which, pl.ds(q * piece, piece)],
                sems.at[which, q],
            )
            copy.start()
            copies.append(copy)
    cols = pl.ds(pl.multiple_of(half * depth, depth), depth)
    x_high, x_low = split(x_ref[:, cols])
    total = first_ref[...] if has_first else None
    for copy in copies[:PARTS]:
        copy.wait()
    w_high, w_low = split(held_ref[0])
    term = product(x_high, x_low, w_high, w_low)
    total = term if total is None else total + term
    base = 0
    for part_ref in part_refs:
        count = part_ref.shape[0]
        part_ref[...] = total[base : base + count]
        base += count
    for copy in copies[PARTS:]:
        copy.wait()
    o_high, o_low = split(held_ref[1])
    high_ref[...] = o_high
    low_ref[...] = o_low


def last_kernel(got_ref, high0_ref, low0_ref, high1_ref, low1_ref, part_ref, out_ref):
    depth = high0_ref.shape[0]
    total = part_ref[...]
    for n, (high_ref, low_ref) in enumerate(((high0_ref, low0_ref), (high1_ref, low1_ref))):
        total = total + product(*split(got_ref[:, n * depth : (n + 1) * depth]), high_ref[...], low_ref[...])
    put(out_ref, total)


def put(out_ref, total):
    tiles = total.shape[1] // LANES
    block = R * tiles
    for r in range(R):
        for h in range(2):
            row = (r * 2 + h) * Z
            for t in range(tiles):
                rows = total[row : row + Z, t * LANES : (t + 1) * LANES]
                out_ref[pl.ds(h * block + t * R + r, Z, 2 * block), :] = pltpu.roll(rows, Z - START_Z, 0)


def add_kernel(got_ref, part_ref, *out_refs):
    for n, out_ref in enumerate(out_refs):
        rows = pl.ds(n * PIECE, PIECE)
        put(out_ref, got_ref[rows, :] + part_ref[rows, :])


def gather_kernel(*refs):
    *in_refs, out_ref = refs
    block = in_refs[0].shape[0] // (2 * Z)
    for j, in_ref in enumerate(in_refs):
        for n in range(2 * Z):
            out_ref[pl.ds((n * len(in_refs) + j) * block, block), :] = in_ref[pl.ds(n * block, block), :]


def merge_kernel(moved_ref, second_ref, out_ref):
    block = out_ref.shape[0] // (2 * Y * Z)
    _, here_y, _ = here()
    for dy in range(Y):
        y = lax.rem(here_y - dy + Y, Y)
        for n in range(2 * Z):
            if dy == FIRST:
                value = moved_ref[pl.ds(n * block, block), :]
            else:
                value = second_ref[pl.ds((n * len(SECOND) + SECOND.index(dy)) * block, block), :]
            z, h = (n // 2 + START_Z) % Z, n % 2
            out_ref[pl.ds(pl.multiple_of(((z * Y + y) * 2 + h) * block, block), block), :] = value


def call(kernel, name, out_shape, in_specs, scratch=(), flops=1000):
    return pl.pallas_call(
        kernel,
        out_shape=out_shape,
        in_specs=in_specs,
        out_specs=jax.tree.map(lambda _: vmem(), out_shape),
        scratch_shapes=list(scratch),
        compiler_params=pltpu.CompilerParams(vmem_limit_bytes=24 * 2**20),
        cost_estimate=pl.CostEstimate(flops=flops, bytes_accessed=1000, transcendentals=0),
        name=name,
    )


def on_device(n_pair, groups, amplitudes, domain_mask, integrals):
    f32, bf16 = jnp.float32, jnp.bfloat16

    def of(*shape, dtype=f32):
        return jax.ShapeDtypeStruct(shape, dtype)

    rows, width = amplitudes.shape[1:]
    depth, columns = integrals.shape[1:]
    kept = rows // 2
    dests = kept // R
    tiles = columns // LANES
    swap = [(p, p ^ 1) for p in range(n_pair)]
    other = lax.ppermute(integrals, "blk", [(0, 1), (1, 0)])
    n_tiles = width // LANES
    mask_scratch = pltpu.VMEM(domain_mask.shape[1:], jnp.int32)
    send0 = call(
        first_kernel,
        "first",
        of(PIECE, width),
        [hbm(), hbm()],
        [
            pltpu.VMEM((n_tiles, Z, X * R, LANES), f32),
            mask_scratch,
            pltpu.SemaphoreType.DMA((n_tiles + 1,)),
        ],
    )(in_hbm(amplitudes.reshape(Z, Y, X * R, width)), in_hbm(domain_mask))
    got0 = lax.ppermute(send0, "pair", swap)
    rest = call(
        rest_kernel,
        "rest",
        of(7 * PIECE, width),
        [hbm(), hbm(), pl.BlockSpec(memory_space=pl.ANY)],
        [pltpu.VMEM((n_tiles, rows, LANES), f32), mask_scratch, pltpu.SemaphoreType.DMA((n_tiles + 1,))],
    )(in_hbm(amplitudes), in_hbm(domain_mask), send0)

    halves_w = [of(depth, columns, dtype=bf16)] * 2
    scratch = [pltpu.VMEM((2, depth, columns), f32), pltpu.SemaphoreType.DMA((2, PARTS))]
    part, high0, low0 = call(
        functools.partial(own_kernel, False),
        "own_near",
        [of(7 * PIECE, columns)] + halves_w,
        [vmem(), hbm()],
        scratch,
    )(rest, in_hbm(integrals))
    part0, *parts, high1, low1 = call(
        functools.partial(own_kernel, True),
        "own_far",
        [of(n * PIECE, columns) for n in (1, 2, 1, 2, 1)] + halves_w,
        [vmem(), hbm(), vmem()],
        scratch,
    )(rest, other, part)
    part_moved, part_own, send_moved, send_own = parts
    send_moved, send_own, _ = lax.optimization_barrier((send_moved, send_own, got0))
    got_moved = lax.ppermute(send_moved, "pair", swap)
    got_own = lax.ppermute(send_own, "pair", swap)

    def along_y(value, dy):
        perm = []
        for p in range(n_pair):
            pz, py, px = p // (X * Y), p // X % Y, p % X
            perm.append((p, (pz * Y + (py + dy) % Y) * X + px))
        return lax.ppermute(value, "pair", perm)

    def across(block):
        out = lax.all_to_all(
            block.reshape(2 * Z, -1, LANES),
            "pair",
            split_axis=0,
            concat_axis=0,
            tiled=True,
            axis_index_groups=groups,
        )
        return out.reshape(-1, LANES)

    piece = of(PIECE * tiles, LANES)
    back0 = across(call(last_kernel, "last", piece, [vmem()] * 6)(got0, high0, low0, high1, low1, part0))
    values = call(add_kernel, "add_moved", [piece] * 2, [vmem()] * 2)(got_moved, part_moved)
    pieces = [along_y(value, dy) for value, dy in zip(values, MOVED)]
    pieces += call(add_kernel, "add_own", [piece], [vmem()] * 2, (), ADD_FLOPS)(got_own, part_own)
    block1 = call(gather_kernel, "gather", of(len(SECOND) * PIECE * tiles, LANES), [vmem()] * len(pieces))(*pieces)
    back1 = across(block1)
    moved = along_y(back0, FIRST)
    whole = call(merge_kernel, "merge", of(dests * R * tiles, LANES), [vmem()] * 2)(moved, back1)
    return whole.reshape(dests, tiles, R, LANES).transpose(0, 2, 1, 3).reshape(dests, R, columns)


def solution(mesh):
    n_pair = mesh.shape["pair"]
    groups = [
        [((z + START_Z) % Z * Y + y) * X + x for z in range(Z) for x in pair] for y in range(Y) for pair in ((0, 3), (1, 2))
    ]
    return jax.shard_map(
        functools.partial(on_device, n_pair, groups),
        mesh=mesh,
        in_specs=(P("pair", "blk", None), P("pair", "blk", None), P(None, "blk", None)),
        out_specs=P(None, ("blk", "pair"), None),
        check_vma=False,
    )
```

```python
import functools
import jax
import jax.numpy as jnp
from jax import lax
from jax.experimental import pallas as pl
from jax.experimental.pallas import tpu as pltpu
from jax.sharding import PartitionSpec as P

TILE = 64
LANES = 128
X = 4
Y = 4
Z = 8
R = 4
ALL, LOW, HIGH = (0, 1, 2, 3), (0, 1), (2, 3)
FIRST = ((2, ALL), (3, LOW))
MOVED = ((1, ALL), (3, HIGH))
OWN = ((0, ALL),)
SECOND = MOVED + OWN
PARTS = 4
ADD_FLOPS = 10**11
START_Z = 5


def vmem():
    return pl.BlockSpec(memory_space=pltpu.VMEM)


def hbm():
    return pl.BlockSpec(memory_space=pltpu.HBM)


def in_hbm(value):
    return pltpu.with_memory_space_constraint(value, pltpu.HBM)


def count(pieces):
    return sum(2 * Z * len(rs) for _, rs in pieces)


def here():
    me = lax.axis_index("pair")
    return lax.rem(me, X), lax.rem(lax.div(me, X), Y), lax.axis_index("blk")


def split(value):
    high = value.astype(jnp.bfloat16)
    low = (value - high.astype(jnp.float32)).astype(jnp.bfloat16)
    return high, low


def dot(a, b):
    return jnp.dot(a, b, preferred_element_type=jnp.float32)


def product(a_high, a_low, b_high, b_low):
    rows = a_high.shape[0]
    both = dot(jnp.concatenate([a_high, a_low], axis=0), b_high)
    return both[:rows] + (both[rows:] + dot(a_high, b_low))


def tile_rows(mask_ref, shift, width):
    tiles = mask_ref.shape[1]
    column = lax.div(lax.broadcasted_iota(jnp.int32, (tiles, width), 1), TILE)
    spread = lax.rem(column + shift, tiles) == lax.broadcasted_iota(jnp.int32, (tiles, width), 0)
    return dot(mask_ref[...].astype(jnp.float32), spread.astype(jnp.float32))


def first_kernel(t_ref, mask_ref, out_ref, held_ref, mask_held, sems):
    width = t_ref.shape[3]
    tiles = width // LANES
    x, y, blk = here()
    partner = x + 1 - 2 * lax.rem(x, 2)
    mask_copy = pltpu.make_async_copy(mask_ref.at[0], mask_held, sems.at[len(FIRST) * tiles])
    mask_copy.start()
    copies = []
    for t in range(tiles):
        lanes = pl.multiple_of(lax.rem(t + blk * (tiles // 2), tiles) * LANES, LANES)
        for n, (dy, _) in enumerate(FIRST):
            copy = pltpu.make_async_copy(
                t_ref.at[:, lax.rem(y + dy, Y), :, pl.ds(lanes, LANES)],
                held_ref.at[t, n],
                sems.at[t * len(FIRST) + n],
            )
            copy.start()
            copies.append(copy)
    mask_copy.wait()
    mask = tile_rows(mask_held, blk * (mask_ref.shape[2] // 2), width)
    for t in range(tiles):
        cols = pl.ds(t * LANES, LANES)
        m = mask[:, t * LANES : (t + 1) * LANES]
        at = 0
        for n, (_, rs) in enumerate(FIRST):
            copies[t * len(FIRST) + n].wait()
            rows = held_ref.at[t, n].reshape(Z * X * R, LANES)
            for r in rs:
                for h in range(2):
                    value = rows[pl.ds(end(partner, h) * R + r, Z, X * R), :]
                    out_ref[pl.ds(at, Z), cols] = value * m
                    at += Z


def end(x, h):
    outer = (x == 0) | (x == X - 1)
    return jnp.where(outer, h * (X - 1), 1 + h)


def rest_kernel(t_ref, mask_ref, after_ref, rest_ref, held_ref, mask_held, sems):
    del after_ref
    rows, width = t_ref.shape[1:]
    x, y, blk = here()
    partner = x + 1 - 2 * lax.rem(x, 2)
    plane = X * Y * R
    tiles = width // LANES
    mask_copy = pltpu.make_async_copy(mask_ref.at[0], mask_held, sems.at[tiles])
    mask_copy.start()
    copies = []
    for t in range(tiles):
        copy = pltpu.make_async_copy(t_ref.at[0, :, pl.ds(t * LANES, LANES)], held_ref.at[t], sems.at[t])
        copy.start()
        copies.append(copy)
    mask_copy.wait()
    mask = tile_rows(mask_held, 0, width)
    wanted = [(piece, x) for piece in FIRST + SECOND] + [(piece, partner) for piece in SECOND]
    for t in range(tiles):
        copies[t].wait()
        cols = pl.ds(t * LANES, LANES)
        m = mask[:, t * LANES : (t + 1) * LANES]
        at = 0
        for (dy, rs), device in wanted:
            for r in rs:
                for h in range(2):
                    base = (lax.rem(y + dy, Y) * X + end(device, h)) * R
                    rest_ref[pl.ds(at, Z), cols] = held_ref[t, pl.ds(base + r, Z, plane), :] * m
                    at += Z


def own_kernel(has_first, x_ref, w_ref, *refs):
    x, _, blk = here()
    k = lax.rem(x, 2)
    half = 1 - blk if has_first else blk
    first_ref = refs[0] if has_first else None
    *part_refs, high_ref, low_ref, held_ref, sems = refs[has_first:]
    depth = w_ref.shape[1]
    piece = depth // PARTS
    copies = []
    for which, of in enumerate((k, 1 - k)):
        for q in range(PARTS):
            copy = pltpu.make_async_copy(
                w_ref.at[of, pl.ds(q * piece, piece)],
                held_ref.at[which, pl.ds(q * piece, piece)],
                sems.at[which, q],
            )
            copy.start()
            copies.append(copy)
    cols = pl.ds(pl.multiple_of(half * depth, depth), depth)
    x_high, x_low = split(x_ref[:, cols])
    total = first_ref[...] if has_first else None
    for copy in copies[:PARTS]:
        copy.wait()
    w_high, w_low = split(held_ref[0])
    term = product(x_high, x_low, w_high, w_low)
    total = term if total is None else total + term
    base = 0
    for part_ref in part_refs:
        count = part_ref.shape[0]
        part_ref[...] = total[base : base + count]
        base += count
    for copy in copies[PARTS:]:
        copy.wait()
    o_high, o_low = split(held_ref[1])
    high_ref[...] = o_high
    low_ref[...] = o_low


def last_kernel(got_ref, high0_ref, low0_ref, high1_ref, low1_ref, part_ref, out_ref):
    depth = high0_ref.shape[0]
    total = part_ref[...]
    for n, (high_ref, low_ref) in enumerate(((high0_ref, low0_ref), (high1_ref, low1_ref))):
        total = total + product(*split(got_ref[:, n * depth : (n + 1) * depth]), high_ref[...], low_ref[...])
    put([out_ref], total, FIRST, True)


def put(out_refs, total, pieces, joined):
    tiles = total.shape[1] // LANES
    whole = sum(len(rs) for _, rs in pieces) * tiles
    row, start = 0, 0
    for n, (_, rs) in enumerate(pieces):
        out_ref = out_refs[0 if joined else n]
        block = whole if joined else len(rs) * tiles
        for j in range(len(rs)):
            for h in range(2):
                for t in range(tiles):
                    rows = pltpu.roll(total[row : row + Z, t * LANES : (t + 1) * LANES], Z - START_Z, 0)
                    out_ref[pl.ds(h * block + start + t * len(rs) + j, Z, 2 * block), :] = rows
                row += Z
        start += len(rs) * tiles if joined else 0


def moved_kernel(got_ref, part_ref, *out_refs):
    put(out_refs, got_ref[...] + part_ref[...], MOVED, False)


def own_sum_kernel(got_ref, part_ref, *out_refs):
    put(out_refs, got_ref[...] + part_ref[...], OWN, False)


def turn_kernel(in_ref, *out_refs):
    whole, start = in_ref.shape[0] // (2 * Z), 0
    for out_ref in out_refs:
        block = out_ref.shape[0] // (2 * Z)
        for n in range(2 * Z):
            out_ref[pl.ds(n * block, block), :] = in_ref[pl.ds(n * whole + start, block), :]
        start += block


def gather_kernel(*refs):
    *in_refs, out_ref = refs
    whole, start = out_ref.shape[0] // (2 * Z), 0
    for in_ref in in_refs:
        block = in_ref.shape[0] // (2 * Z)
        for n in range(2 * Z):
            out_ref[pl.ds(n * whole + start, block), :] = in_ref[pl.ds(n * block, block), :]
        start += block


def merge_kernel(*refs):
    *moved_refs, second_ref, out_ref = refs
    block = out_ref.shape[0] // (2 * Y * Z)
    tiles = block // R
    whole = second_ref.shape[0] // (2 * Z)
    _, here_y, _ = here()
    sources = [(dy, rs, ref, len(rs) * tiles, 0) for (dy, rs), ref in zip(FIRST, moved_refs)]
    start = 0
    for dy, rs in SECOND:
        sources.append((dy, rs, second_ref, whole, start))
        start += len(rs) * tiles
    for dy, rs, ref, pitch, start in sources:
        y = lax.rem(here_y - dy + Y, Y)
        for n in range(2 * Z):
            z, h = (n // 2 + START_Z) % Z, n % 2
            to = pl.multiple_of(((z * Y + y) * 2 + h) * block, block)
            at = n * pitch + start
            if len(rs) == R:
                out_ref[pl.ds(to, block), :] = ref[pl.ds(at, block), :]
            else:
                for j, r in enumerate(rs):
                    out_ref[pl.ds(to + r, tiles, R), :] = ref[pl.ds(at + j, tiles, len(rs)), :]


def call(kernel, name, out_shape, in_specs, scratch=(), flops=1000):
    return pl.pallas_call(
        kernel,
        out_shape=out_shape,
        in_specs=in_specs,
        out_specs=jax.tree.map(lambda _: vmem(), out_shape),
        scratch_shapes=list(scratch),
        compiler_params=pltpu.CompilerParams(vmem_limit_bytes=24 * 2**20),
        cost_estimate=pl.CostEstimate(flops=flops, bytes_accessed=1000, transcendentals=0),
        name=name,
    )


def on_device(n_pair, groups, amplitudes, domain_mask, integrals):
    f32, bf16 = jnp.float32, jnp.bfloat16

    def of(*shape, dtype=f32):
        return jax.ShapeDtypeStruct(shape, dtype)

    rows, width = amplitudes.shape[1:]
    depth, columns = integrals.shape[1:]
    kept = rows // 2
    dests = kept // R
    tiles = columns // LANES
    swap = [(p, p ^ 1) for p in range(n_pair)]
    other = lax.ppermute(integrals, "blk", [(0, 1), (1, 0)])
    n_tiles = width // LANES
    n_rest = count(FIRST) + 2 * count(SECOND)
    mask_scratch = pltpu.VMEM(domain_mask.shape[1:], jnp.int32)
    send0 = call(
        first_kernel,
        "first",
        of(count(FIRST), width),
        [hbm(), hbm()],
        [
            pltpu.VMEM((n_tiles, len(FIRST), Z, X * R, LANES), f32),
            mask_scratch,
            pltpu.SemaphoreType.DMA((len(FIRST) * n_tiles + 1,)),
        ],
    )(in_hbm(amplitudes.reshape(Z, Y, X * R, width)), in_hbm(domain_mask))
    got0 = lax.ppermute(send0, "pair", swap)
    rest = call(
        rest_kernel,
        "rest",
        of(n_rest, width),
        [hbm(), hbm(), pl.BlockSpec(memory_space=pl.ANY)],
        [pltpu.VMEM((n_tiles, rows, LANES), f32), mask_scratch, pltpu.SemaphoreType.DMA((n_tiles + 1,))],
    )(in_hbm(amplitudes), in_hbm(domain_mask), send0)

    halves_w = [of(depth, columns, dtype=bf16)] * 2
    scratch = [pltpu.VMEM((2, depth, columns), f32), pltpu.SemaphoreType.DMA((2, PARTS))]
    part, high0, low0 = call(
        functools.partial(own_kernel, False),
        "own_near",
        [of(n_rest, columns)] + halves_w,
        [vmem(), hbm()],
        scratch,
    )(rest, in_hbm(integrals))
    part0, *parts, high1, low1 = call(
        functools.partial(own_kernel, True),
        "own_far",
        [of(count(pieces), columns) for pieces in (FIRST, MOVED, OWN, MOVED, OWN)] + halves_w,
        [vmem(), hbm(), vmem()],
        scratch,
    )(rest, other, part)
    part_moved, part_own, send_moved, send_own = parts
    got_moved = lax.ppermute(send_moved, "pair", swap)
    got_own = lax.ppermute(send_own, "pair", swap)

    def along_y(value, dy):
        perm = []
        for p in range(n_pair):
            pz, py, px = p // (X * Y), p // X % Y, p % X
            perm.append((p, (pz * Y + (py + dy) % Y) * X + px))
        return lax.ppermute(value, "pair", perm)

    def across(block):
        out = lax.all_to_all(
            block.reshape(2 * Z, -1, LANES),
            "pair",
            split_axis=0,
            concat_axis=0,
            tiled=True,
            axis_index_groups=groups,
        )
        return out.reshape(-1, LANES)


    def blocks(pieces):
        return [of(count((piece,)) * tiles, LANES) for piece in pieces]

    block0 = call(last_kernel, "last", of(count(FIRST) * tiles, LANES), [vmem()] * 6)(
        got0, high0, low0, high1, low1, part0
    )
    back0 = across(block0)
    pieces = call(moved_kernel, "add_moved", blocks(MOVED), [vmem()] * 2)(got_moved, part_moved)
    pieces = [along_y(value, dy) for value, (dy, _) in zip(pieces, MOVED)]
    pieces += call(own_sum_kernel, "add_own", blocks(OWN), [vmem()] * 2, (), ADD_FLOPS)(got_own, part_own)
    block1 = call(gather_kernel, "gather", of(count(SECOND) * tiles, LANES), [vmem()] * len(pieces))(*pieces)
    back1 = across(block1)
    moved = call(turn_kernel, "turn", blocks(FIRST), [vmem()])(back0)
    moved = [along_y(value, dy) for value, (dy, _) in zip(moved, FIRST)]
    whole = call(merge_kernel, "merge", of(dests * R * tiles, LANES), [vmem()] * (len(moved) + 1))(*moved, back1)
    return whole.reshape(dests, tiles, R, LANES).transpose(0, 2, 1, 3).reshape(dests, R, columns)


def solution(mesh):
    n_pair = mesh.shape["pair"]
    groups = [
        [((z + START_Z) % Z * Y + y) * X + x for z in range(Z) for x in pair] for y in range(Y) for pair in ((0, 3), (1, 2))
    ]
    return jax.shard_map(
        functools.partial(on_device, n_pair, groups),
        mesh=mesh,
        in_specs=(P("pair", "blk", None), P("pair", "blk", None), P(None, "blk", None)),
        out_specs=P(None, ("blk", "pair"), None),
        check_vma=False,
    )
```

```python
import functools
import jax
import jax.numpy as jnp
from jax import lax
from jax.experimental import pallas as pl
from jax.experimental.pallas import tpu as pltpu
from jax.sharding import PartitionSpec as P

TILE = 64
LANES = 128
X = 4
Y = 4
Z = 8
R = 4
ALL = (0, 1, 2, 3)
FIRST = ((2, ALL), (0, (0, 1)))
SECOND = ((1, ALL), (3, ALL), (0, (2, 3)))
PARTS = 4
ADD_FLOPS = 10**11
START_Z = 5


def vmem():
    return pl.BlockSpec(memory_space=pltpu.VMEM)


def hbm():
    return pl.BlockSpec(memory_space=pltpu.HBM)


def in_hbm(value):
    return pltpu.with_memory_space_constraint(value, pltpu.HBM)


def count(pieces):
    return sum(2 * Z * len(rs) for _, rs in pieces)


def here():
    me = lax.axis_index("pair")
    return lax.rem(me, X), lax.rem(lax.div(me, X), Y), lax.axis_index("blk")


def split(value):
    high = value.astype(jnp.bfloat16)
    low = (value - high.astype(jnp.float32)).astype(jnp.bfloat16)
    return high, low


def dot(a, b):
    return jnp.dot(a, b, preferred_element_type=jnp.float32)


def product(a_high, a_low, b_high, b_low):
    rows = a_high.shape[0]
    both = dot(jnp.concatenate([a_high, a_low], axis=0), b_high)
    return both[:rows] + (both[rows:] + dot(a_high, b_low))


def tile_rows(mask_ref, shift, width):
    tiles = mask_ref.shape[1]
    column = lax.div(lax.broadcasted_iota(jnp.int32, (tiles, width), 1), TILE)
    spread = lax.rem(column + shift, tiles) == lax.broadcasted_iota(jnp.int32, (tiles, width), 0)
    return dot(mask_ref[...].astype(jnp.float32), spread.astype(jnp.float32))


def first_kernel(t_ref, mask_ref, out_ref, held_ref, mask_held, sems):
    width = t_ref.shape[3]
    tiles = width // LANES
    x, y, blk = here()
    partner = x + 1 - 2 * lax.rem(x, 2)
    mask_copy = pltpu.make_async_copy(mask_ref.at[0], mask_held, sems.at[len(FIRST) * tiles])
    mask_copy.start()
    copies = []
    for t in range(tiles):
        lanes = pl.multiple_of(lax.rem(t + blk * (tiles // 2), tiles) * LANES, LANES)
        for n, (dy, _) in enumerate(FIRST):
            copy = pltpu.make_async_copy(
                t_ref.at[:, lax.rem(y + dy, Y), :, pl.ds(lanes, LANES)],
                held_ref.at[t, n],
                sems.at[t * len(FIRST) + n],
            )
            copy.start()
            copies.append(copy)
    mask_copy.wait()
    mask = tile_rows(mask_held, blk * (mask_ref.shape[2] // 2), width)
    for t in range(tiles):
        cols = pl.ds(t * LANES, LANES)
        m = mask[:, t * LANES : (t + 1) * LANES]
        at = 0
        for n, (_, rs) in enumerate(FIRST):
            copies[t * len(FIRST) + n].wait()
            rows = held_ref.at[t, n].reshape(Z * X * R, LANES)
            for r in rs:
                for h in range(2):
                    value = rows[pl.ds(end(partner, h) * R + r, Z, X * R), :]
                    out_ref[pl.ds(at, Z), cols] = value * m
                    at += Z


def end(x, h):
    outer = (x == 0) | (x == X - 1)
    return jnp.where(outer, h * (X - 1), 1 + h)


def near_kernel(
    t_ref, mask_ref, w_ref, after_ref, rest_ref, part_ref, high_ref, low_ref, held_ref, mask_held, w_held, sems, w_sems
):
    del after_ref
    rows, width = t_ref.shape[1:]
    x, y, blk = here()
    partner = x + 1 - 2 * lax.rem(x, 2)
    plane = X * Y * R
    tiles = width // LANES
    mask_copy = pltpu.make_async_copy(mask_ref.at[0], mask_held, sems.at[tiles])
    mask_copy.start()
    copies = []
    for t in range(tiles):
        copy = pltpu.make_async_copy(t_ref.at[0, :, pl.ds(t * LANES, LANES)], held_ref.at[t], sems.at[t])
        copy.start()
        copies.append(copy)
    w_copies = start_weights(w_ref, w_held, w_sems)
    mask_copy.wait()
    mask = tile_rows(mask_held, 0, width)
    wanted = [(piece, x) for piece in FIRST + SECOND] + [(piece, partner) for piece in SECOND]
    for t in range(tiles):
        copies[t].wait()
        cols = pl.ds(t * LANES, LANES)
        m = mask[:, t * LANES : (t + 1) * LANES]
        at = 0
        for (dy, rs), device in wanted:
            for r in rs:
                for h in range(2):
                    base = (lax.rem(y + dy, Y) * X + end(device, h)) * R
                    rest_ref[pl.ds(at, Z), cols] = held_ref[t, pl.ds(base + r, Z, plane), :] * m
                    at += Z
    contract(w_copies, blk, rest_ref, None, [part_ref], high_ref, low_ref, w_held)


def start_weights(w_ref, held_ref, sems):
    k = lax.rem(here()[0], 2)
    piece = w_ref.shape[1] // PARTS
    copies = []
    for which, of in enumerate((k, 1 - k)):
        for q in range(PARTS):
            copy = pltpu.make_async_copy(
                w_ref.at[of, pl.ds(q * piece, piece)],
                held_ref.at[which, pl.ds(q * piece, piece)],
                sems.at[which, q],
            )
            copy.start()
            copies.append(copy)
    return copies


def contract(copies, half, x_ref, first_ref, part_refs, high_ref, low_ref, held_ref):
    depth = held_ref.shape[1]
    x_high, x_low = split(x_ref[:, pl.ds(pl.multiple_of(half * depth, depth), depth)])
    for copy in copies[:PARTS]:
        copy.wait()
    total = product(x_high, x_low, *split(held_ref[0]))
    if first_ref is not None:
        total = first_ref[...] + total
    base = 0
    for part_ref in part_refs:
        size = part_ref.shape[0]
        part_ref[...] = total[base : base + size]
        base += size
    for copy in copies[PARTS:]:
        copy.wait()
    o_high, o_low = split(held_ref[1])
    high_ref[...] = o_high
    low_ref[...] = o_low


def far_kernel(x_ref, w_ref, first_ref, *refs):
    *part_refs, high_ref, low_ref, held_ref, sems = refs
    copies = start_weights(w_ref, held_ref, sems)
    contract(copies, 1 - here()[2], x_ref, first_ref, part_refs, high_ref, low_ref, held_ref)


def last_kernel(got_ref, high0_ref, low0_ref, high1_ref, low1_ref, part_ref, out_ref):
    depth = high0_ref.shape[0]
    total = part_ref[...]
    for n, (high_ref, low_ref) in enumerate(((high0_ref, low0_ref), (high1_ref, low1_ref))):
        total = total + product(*split(got_ref[:, n * depth : (n + 1) * depth]), high_ref[...], low_ref[...])
    put([out_ref], total, FIRST, True)


def put(out_refs, total, pieces, joined):
    tiles = total.shape[1] // LANES
    whole = sum(len(rs) for _, rs in pieces) * tiles
    row, start = 0, 0
    for n, (_, rs) in enumerate(pieces):
        out_ref = out_refs[0 if joined else n]
        block = whole if joined else len(rs) * tiles
        for j in range(len(rs)):
            for h in range(2):
                for t in range(tiles):
                    rows = pltpu.roll(total[row : row + Z, t * LANES : (t + 1) * LANES], Z - START_Z, 0)
                    out_ref[pl.ds(h * block + start + t * len(rs) + j, Z, 2 * block), :] = rows
                row += Z
        start += len(rs) * tiles if joined else 0


def sum_kernel(piece, got_ref, part_ref, out_ref):
    put([out_ref], got_ref[...] + part_ref[...], (piece,), False)


def turn_kernel(in_ref, *out_refs):
    whole, start = in_ref.shape[0] // (2 * Z), 0
    for out_ref in out_refs:
        block = out_ref.shape[0] // (2 * Z)
        for n in range(2 * Z):
            out_ref[pl.ds(n * block, block), :] = in_ref[pl.ds(n * whole + start, block), :]
        start += block


def gather_kernel(*refs):
    *in_refs, out_ref = refs
    whole, start = out_ref.shape[0] // (2 * Z), 0
    for in_ref in in_refs:
        block = in_ref.shape[0] // (2 * Z)
        for n in range(2 * Z):
            out_ref[pl.ds(n * whole + start, block), :] = in_ref[pl.ds(n * block, block), :]
        start += block


def merge_kernel(*refs):
    *moved_refs, second_ref, out_ref = refs
    block = out_ref.shape[0] // (2 * Y * Z)
    tiles = block // R
    whole = second_ref.shape[0] // (2 * Z)
    _, here_y, _ = here()
    sources = [(dy, rs, ref, len(rs) * tiles, 0) for (dy, rs), ref in zip(FIRST, moved_refs)]
    start = 0
    for dy, rs in SECOND:
        sources.append((dy, rs, second_ref, whole, start))
        start += len(rs) * tiles
    for dy, rs, ref, pitch, start in sources:
        y = lax.rem(here_y - dy + Y, Y)
        for n in range(2 * Z):
            z, h = (n // 2 + START_Z) % Z, n % 2
            to = pl.multiple_of(((z * Y + y) * 2 + h) * block, block)
            at = n * pitch + start
            if len(rs) == R:
                out_ref[pl.ds(to, block), :] = ref[pl.ds(at, block), :]
            else:
                for j, r in enumerate(rs):
                    out_ref[pl.ds(to + r, tiles, R), :] = ref[pl.ds(at + j, tiles, len(rs)), :]


def call(kernel, name, out_shape, in_specs, scratch=(), flops=1000):
    return pl.pallas_call(
        kernel,
        out_shape=out_shape,
        in_specs=in_specs,
        out_specs=jax.tree.map(lambda _: vmem(), out_shape),
        scratch_shapes=list(scratch),
        compiler_params=pltpu.CompilerParams(vmem_limit_bytes=24 * 2**20),
        cost_estimate=pl.CostEstimate(flops=flops, bytes_accessed=1000, transcendentals=0),
        name=name,
    )


def on_device(n_pair, groups, amplitudes, domain_mask, integrals):
    f32, bf16 = jnp.float32, jnp.bfloat16

    def of(*shape, dtype=f32):
        return jax.ShapeDtypeStruct(shape, dtype)

    rows, width = amplitudes.shape[1:]
    depth, columns = integrals.shape[1:]
    kept = rows // 2
    dests = kept // R
    tiles = columns // LANES
    swap = [(p, p ^ 1) for p in range(n_pair)]
    other = lax.ppermute(integrals, "blk", [(0, 1), (1, 0)])
    n_tiles = width // LANES
    n_rest = count(FIRST) + 2 * count(SECOND)
    mask_scratch = pltpu.VMEM(domain_mask.shape[1:], jnp.int32)
    send0 = call(
        first_kernel,
        "first",
        of(count(FIRST), width),
        [hbm(), hbm()],
        [
            pltpu.VMEM((n_tiles, len(FIRST), Z, X * R, LANES), f32),
            mask_scratch,
            pltpu.SemaphoreType.DMA((len(FIRST) * n_tiles + 1,)),
        ],
    )(in_hbm(amplitudes.reshape(Z, Y, X * R, width)), in_hbm(domain_mask))
    got0 = lax.ppermute(send0, "pair", swap)
    halves_w = [of(depth, columns, dtype=bf16)] * 2
    scratch = [pltpu.VMEM((2, depth, columns), f32), pltpu.SemaphoreType.DMA((2, PARTS))]
    rest, part, high0, low0 = call(
        near_kernel,
        "near",
        [of(n_rest, width), of(n_rest, columns)] + halves_w,
        [hbm(), hbm(), hbm(), pl.BlockSpec(memory_space=pl.ANY)],
        [pltpu.VMEM((n_tiles, rows, LANES), f32), mask_scratch, scratch[0], pltpu.SemaphoreType.DMA((n_tiles + 1,)), scratch[1]],
    )(in_hbm(amplitudes), in_hbm(domain_mask), in_hbm(integrals), send0)
    sizes = [count((piece,)) for piece in SECOND]
    part0, *parts, high1, low1 = call(
        far_kernel,
        "far",
        [of(n, columns) for n in [count(FIRST)] + sizes + sizes] + halves_w,
        [vmem(), hbm(), vmem()],
        scratch,
    )(rest, other, part)
    parts, sends = parts[: len(SECOND)], parts[len(SECOND) :]
    got = [lax.ppermute(send, "pair", swap) for send in sends]

    def along_y(value, dy):
        perm = []
        for p in range(n_pair):
            pz, py, px = p // (X * Y), p // X % Y, p % X
            perm.append((p, (pz * Y + (py + dy) % Y) * X + px))
        return lax.ppermute(value, "pair", perm)

    def across(block):
        out = lax.all_to_all(
            block.reshape(2 * Z, -1, LANES),
            "pair",
            split_axis=0,
            concat_axis=0,
            tiled=True,
            axis_index_groups=groups,
        )
        return out.reshape(-1, LANES)


    def blocks(pieces):
        return [of(count((piece,)) * tiles, LANES) for piece in pieces]

    block0 = call(last_kernel, "last", of(count(FIRST) * tiles, LANES), [vmem()] * 6)(
        got0, high0, low0, high1, low1, part0
    )
    back0 = across(block0)
    pieces = []
    for n, (dy, rs) in enumerate(SECOND):
        value = call(
            functools.partial(sum_kernel, (dy, rs)),
            "sum",
            of(sizes[n] * tiles, LANES),
            [vmem()] * 2,
            (),
            1000 if dy else ADD_FLOPS,
        )(got[n], parts[n])
        pieces.append(along_y(value, dy) if dy else value)
    block1 = call(gather_kernel, "gather", of(count(SECOND) * tiles, LANES), [vmem()] * len(pieces))(*pieces)
    back1 = across(block1)
    moved = call(turn_kernel, "turn", blocks(FIRST), [vmem()])(back0) if len(FIRST) > 1 else [back0]
    moved = [along_y(value, dy) if dy else value for value, (dy, _) in zip(moved, FIRST)]
    whole = call(merge_kernel, "merge", of(dests * R * tiles, LANES), [vmem()] * (len(moved) + 1))(*moved, back1)
    return whole.reshape(dests, tiles, R, LANES).transpose(0, 2, 1, 3).reshape(dests, R, columns)


def solution(mesh):
    n_pair = mesh.shape["pair"]
    groups = [
        [((z + START_Z) % Z * Y + y) * X + x for z in range(Z) for x in pair] for y in range(Y) for pair in ((0, 3), (1, 2))
    ]
    return jax.shard_map(
        functools.partial(on_device, n_pair, groups),
        mesh=mesh,
        in_specs=(P("pair", "blk", None), P("pair", "blk", None), P(None, "blk", None)),
        out_specs=P(None, ("blk", "pair"), None),
        check_vma=False,
    )
```

```python
import functools
import jax
import jax.numpy as jnp
from jax import lax
from jax.experimental import pallas as pl
from jax.experimental.pallas import tpu as pltpu
from jax.sharding import PartitionSpec as P

TILE = 64
LANES = 128
X = 4
Y = 4
Z = 8
R = 4
ALL = (0, 1, 2, 3)
FIRST = ((2, ALL), (0, (0,)))
SECOND = ((1, ALL), (3, ALL), (0, (1, 2, 3)))
PARTS = 4
ADD_FLOPS = 10**11
START_Z = 5


def vmem():
    return pl.BlockSpec(memory_space=pltpu.VMEM)


def hbm():
    return pl.BlockSpec(memory_space=pltpu.HBM)


def in_hbm(value):
    return pltpu.with_memory_space_constraint(value, pltpu.HBM)


def count(pieces):
    return sum(2 * Z * len(rs) for _, rs in pieces)


def here():
    me = lax.axis_index("pair")
    return lax.rem(me, X), lax.rem(lax.div(me, X), Y), lax.axis_index("blk")


def split(value):
    high = value.astype(jnp.bfloat16)
    low = (value - high.astype(jnp.float32)).astype(jnp.bfloat16)
    return high, low


def dot(a, b):
    return jnp.dot(a, b, preferred_element_type=jnp.float32)


def product(a_high, a_low, b_high, b_low):
    rows = a_high.shape[0]
    both = dot(jnp.concatenate([a_high, a_low], axis=0), b_high)
    return both[:rows] + (both[rows:] + dot(a_high, b_low))


def tile_rows(mask_ref, shift, width):
    tiles = mask_ref.shape[1]
    column = lax.div(lax.broadcasted_iota(jnp.int32, (tiles, width), 1), TILE)
    spread = lax.rem(column + shift, tiles) == lax.broadcasted_iota(jnp.int32, (tiles, width), 0)
    return dot(mask_ref[...].astype(jnp.float32), spread.astype(jnp.float32))


def first_kernel(t_ref, mask_ref, out_ref, held_ref, mask_held, sems):
    width = t_ref.shape[3]
    tiles = width // LANES
    x, y, blk = here()
    partner = x + 1 - 2 * lax.rem(x, 2)
    mask_copy = pltpu.make_async_copy(mask_ref.at[0], mask_held, sems.at[len(FIRST) * tiles])
    mask_copy.start()
    copies = []
    for t in range(tiles):
        lanes = pl.multiple_of(lax.rem(t + blk * (tiles // 2), tiles) * LANES, LANES)
        for n, (dy, _) in enumerate(FIRST):
            copy = pltpu.make_async_copy(
                t_ref.at[:, lax.rem(y + dy, Y), :, pl.ds(lanes, LANES)],
                held_ref.at[t, n],
                sems.at[t * len(FIRST) + n],
            )
            copy.start()
            copies.append(copy)
    mask_copy.wait()
    mask = tile_rows(mask_held, blk * (mask_ref.shape[2] // 2), width)
    for t in range(tiles):
        cols = pl.ds(t * LANES, LANES)
        m = mask[:, t * LANES : (t + 1) * LANES]
        at = 0
        for n, (_, rs) in enumerate(FIRST):
            copies[t * len(FIRST) + n].wait()
            rows = held_ref.at[t, n].reshape(Z * X * R, LANES)
            for r in rs:
                for h in range(2):
                    value = rows[pl.ds(end(partner, h) * R + r, Z, X * R), :]
                    out_ref[pl.ds(at, Z), cols] = value * m
                    at += Z


def end(x, h):
    outer = (x == 0) | (x == X - 1)
    return jnp.where(outer, h * (X - 1), 1 + h)


def near_kernel(
    t_ref, mask_ref, w_ref, after_ref, rest_ref, part_ref, high_ref, low_ref, held_ref, mask_held, w_held, sems, w_sems
):
    del after_ref
    rows, width = t_ref.shape[1:]
    x, y, blk = here()
    partner = x + 1 - 2 * lax.rem(x, 2)
    plane = X * Y * R
    tiles = width // LANES
    mask_copy = pltpu.make_async_copy(mask_ref.at[0], mask_held, sems.at[tiles])
    mask_copy.start()
    copies = []
    for t in range(tiles):
        copy = pltpu.make_async_copy(t_ref.at[0, :, pl.ds(t * LANES, LANES)], held_ref.at[t], sems.at[t])
        copy.start()
        copies.append(copy)
    w_copies = start_weights(w_ref, w_held, w_sems)
    mask_copy.wait()
    mask = tile_rows(mask_held, 0, width)
    wanted = [(piece, x) for piece in FIRST + SECOND] + [(piece, partner) for piece in SECOND]
    for t in range(tiles):
        copies[t].wait()
        cols = pl.ds(t * LANES, LANES)
        m = mask[:, t * LANES : (t + 1) * LANES]
        at = 0
        for (dy, rs), device in wanted:
            for r in rs:
                for h in range(2):
                    base = (lax.rem(y + dy, Y) * X + end(device, h)) * R
                    rest_ref[pl.ds(at, Z), cols] = held_ref[t, pl.ds(base + r, Z, plane), :] * m
                    at += Z
    contract(w_copies, blk, rest_ref, None, [part_ref], high_ref, low_ref, w_held)


def start_weights(w_ref, held_ref, sems):
    k = lax.rem(here()[0], 2)
    piece = w_ref.shape[1] // PARTS
    copies = []
    for which, of in enumerate((k, 1 - k)):
        for q in range(PARTS):
            copy = pltpu.make_async_copy(
                w_ref.at[of, pl.ds(q * piece, piece)],
                held_ref.at[which, pl.ds(q * piece, piece)],
                sems.at[which, q],
            )
            copy.start()
            copies.append(copy)
    return copies


def contract(copies, half, x_ref, first_ref, part_refs, high_ref, low_ref, held_ref):
    depth = held_ref.shape[1]
    x_high, x_low = split(x_ref[:, pl.ds(pl.multiple_of(half * depth, depth), depth)])
    for copy in copies[:PARTS]:
        copy.wait()
    total = product(x_high, x_low, *split(held_ref[0]))
    if first_ref is not None:
        total = first_ref[...] + total
    base = 0
    for part_ref in part_refs:
        size = part_ref.shape[0]
        part_ref[...] = total[base : base + size]
        base += size
    for copy in copies[PARTS:]:
        copy.wait()
    o_high, o_low = split(held_ref[1])
    high_ref[...] = o_high
    low_ref[...] = o_low


def far_kernel(x_ref, w_ref, first_ref, *refs):
    *part_refs, high_ref, low_ref, held_ref, sems = refs
    copies = start_weights(w_ref, held_ref, sems)
    contract(copies, 1 - here()[2], x_ref, first_ref, part_refs, high_ref, low_ref, held_ref)


def last_kernel(got_ref, high0_ref, low0_ref, high1_ref, low1_ref, part_ref, out_ref):
    depth = high0_ref.shape[0]
    total = part_ref[...]
    for n, (high_ref, low_ref) in enumerate(((high0_ref, low0_ref), (high1_ref, low1_ref))):
        total = total + product(*split(got_ref[:, n * depth : (n + 1) * depth]), high_ref[...], low_ref[...])
    put([out_ref], total, FIRST, True)


def put(out_refs, total, pieces, joined):
    tiles = total.shape[1] // LANES
    whole = sum(len(rs) for _, rs in pieces) * tiles
    row, start = 0, 0
    for n, (_, rs) in enumerate(pieces):
        out_ref = out_refs[0 if joined else n]
        block = whole if joined else len(rs) * tiles
        for j in range(len(rs)):
            for h in range(2):
                for t in range(tiles):
                    rows = pltpu.roll(total[row : row + Z, t * LANES : (t + 1) * LANES], Z - START_Z, 0)
                    out_ref[pl.ds(h * block + start + t * len(rs) + j, Z, 2 * block), :] = rows
                row += Z
        start += len(rs) * tiles if joined else 0


def sum_kernel(piece, got_ref, part_ref, out_ref):
    put([out_ref], got_ref[...] + part_ref[...], (piece,), False)


def turn_kernel(in_ref, *out_refs):
    whole, start = in_ref.shape[0] // (2 * Z), 0
    for out_ref in out_refs:
        block = out_ref.shape[0] // (2 * Z)
        for n in range(2 * Z):
            out_ref[pl.ds(n * block, block), :] = in_ref[pl.ds(n * whole + start, block), :]
        start += block


def gather_kernel(*refs):
    *in_refs, out_ref = refs
    whole, start = out_ref.shape[0] // (2 * Z), 0
    for in_ref in in_refs:
        block = in_ref.shape[0] // (2 * Z)
        for n in range(2 * Z):
            out_ref[pl.ds(n * whole + start, block), :] = in_ref[pl.ds(n * block, block), :]
        start += block


def merge_kernel(*refs):
    *moved_refs, second_ref, out_ref = refs
    block = out_ref.shape[0] // (2 * Y * Z)
    tiles = block // R
    whole = second_ref.shape[0] // (2 * Z)
    _, here_y, _ = here()
    sources = [(dy, rs, ref, len(rs) * tiles, 0) for (dy, rs), ref in zip(FIRST, moved_refs)]
    start = 0
    for dy, rs in SECOND:
        sources.append((dy, rs, second_ref, whole, start))
        start += len(rs) * tiles
    for dy, rs, ref, pitch, start in sources:
        y = lax.rem(here_y - dy + Y, Y)
        for n in range(2 * Z):
            z, h = (n // 2 + START_Z) % Z, n % 2
            to = pl.multiple_of(((z * Y + y) * 2 + h) * block, block)
            at = n * pitch + start
            if len(rs) == R:
                out_ref[pl.ds(to, block), :] = ref[pl.ds(at, block), :]
            else:
                for j, r in enumerate(rs):
                    out_ref[pl.ds(to + r, tiles, R), :] = ref[pl.ds(at + j, tiles, len(rs)), :]


def call(kernel, name, out_shape, in_specs, scratch=(), flops=1000):
    return pl.pallas_call(
        kernel,
        out_shape=out_shape,
        in_specs=in_specs,
        out_specs=jax.tree.map(lambda _: vmem(), out_shape),
        scratch_shapes=list(scratch),
        compiler_params=pltpu.CompilerParams(vmem_limit_bytes=24 * 2**20),
        cost_estimate=pl.CostEstimate(flops=flops, bytes_accessed=1000, transcendentals=0),
        name=name,
    )


def on_device(n_pair, groups, amplitudes, domain_mask, integrals):
    f32, bf16 = jnp.float32, jnp.bfloat16

    def of(*shape, dtype=f32):
        return jax.ShapeDtypeStruct(shape, dtype)

    rows, width = amplitudes.shape[1:]
    depth, columns = integrals.shape[1:]
    kept = rows // 2
    dests = kept // R
    tiles = columns // LANES
    swap = [(p, p ^ 1) for p in range(n_pair)]
    other = lax.ppermute(integrals, "blk", [(0, 1), (1, 0)])
    n_tiles = width // LANES
    n_rest = count(FIRST) + 2 * count(SECOND)
    mask_scratch = pltpu.VMEM(domain_mask.shape[1:], jnp.int32)
    send0 = call(
        first_kernel,
        "first",
        of(count(FIRST), width),
        [hbm(), hbm()],
        [
            pltpu.VMEM((n_tiles, len(FIRST), Z, X * R, LANES), f32),
            mask_scratch,
            pltpu.SemaphoreType.DMA((len(FIRST) * n_tiles + 1,)),
        ],
    )(in_hbm(amplitudes.reshape(Z, Y, X * R, width)), in_hbm(domain_mask))
    got0 = lax.ppermute(send0, "pair", swap)
    halves_w = [of(depth, columns, dtype=bf16)] * 2
    scratch = [pltpu.VMEM((2, depth, columns), f32), pltpu.SemaphoreType.DMA((2, PARTS))]
    rest, part, high0, low0 = call(
        near_kernel,
        "near",
        [of(n_rest, width), of(n_rest, columns)] + halves_w,
        [hbm(), hbm(), hbm(), pl.BlockSpec(memory_space=pl.ANY)],
        [pltpu.VMEM((n_tiles, rows, LANES), f32), mask_scratch, scratch[0], pltpu.SemaphoreType.DMA((n_tiles + 1,)), scratch[1]],
    )(in_hbm(amplitudes), in_hbm(domain_mask), in_hbm(integrals), send0)
    sizes = [count((piece,)) for piece in SECOND]
    part0, *parts, high1, low1 = call(
        far_kernel,
        "far",
        [of(n, columns) for n in [count(FIRST)] + sizes + sizes] + halves_w,
        [vmem(), hbm(), vmem()],
        scratch,
    )(rest, other, part)
    parts, sends = parts[: len(SECOND)], parts[len(SECOND) :]
    got = [lax.ppermute(send, "pair", swap) for send in sends]

    def along_y(value, dy):
        perm = []
        for p in range(n_pair):
            pz, py, px = p // (X * Y), p // X % Y, p % X
            perm.append((p, (pz * Y + (py + dy) % Y) * X + px))
        return lax.ppermute(value, "pair", perm)

    def across(block):
        out = lax.all_to_all(
            block.reshape(2 * Z, -1, LANES),
            "pair",
            split_axis=0,
            concat_axis=0,
            tiled=True,
            axis_index_groups=groups,
        )
        return out.reshape(-1, LANES)


    def blocks(pieces):
        return [of(count((piece,)) * tiles, LANES) for piece in pieces]

    block0 = call(last_kernel, "last", of(count(FIRST) * tiles, LANES), [vmem()] * 6)(
        got0, high0, low0, high1, low1, part0
    )
    back0 = across(block0)
    pieces = []
    for n, (dy, rs) in enumerate(SECOND):
        value = call(
            functools.partial(sum_kernel, (dy, rs)),
            "sum",
            of(sizes[n] * tiles, LANES),
            [vmem()] * 2,
            (),
            1000 if dy else ADD_FLOPS,
        )(got[n], parts[n])
        pieces.append(along_y(value, dy) if dy else value)
    block1 = call(gather_kernel, "gather", of(count(SECOND) * tiles, LANES), [vmem()] * len(pieces))(*pieces)
    back1 = across(block1)
    moved = call(turn_kernel, "turn", blocks(FIRST), [vmem()])(back0) if len(FIRST) > 1 else [back0]
    moved = [along_y(value, dy) if dy else value for value, (dy, _) in zip(moved, FIRST)]
    whole = call(merge_kernel, "merge", of(dests * R * tiles, LANES), [vmem()] * (len(moved) + 1))(*moved, back1)
    return whole.reshape(dests, tiles, R, LANES).transpose(0, 2, 1, 3).reshape(dests, R, columns)


def solution(mesh):
    n_pair = mesh.shape["pair"]
    groups = [
        [((z + START_Z) % Z * Y + y) * X + x for z in range(Z) for x in pair] for y in range(Y) for pair in ((0, 3), (1, 2))
    ]
    return jax.shard_map(
        functools.partial(on_device, n_pair, groups),
        mesh=mesh,
        in_specs=(P("pair", "blk", None), P("pair", "blk", None), P(None, "blk", None)),
        out_specs=P(None, ("blk", "pair"), None),
        check_vma=False,
    )
```

```python
import functools
import jax
import jax.numpy as jnp
from jax import lax
from jax.experimental import pallas as pl
from jax.experimental.pallas import tpu as pltpu
from jax.sharding import PartitionSpec as P

TILE = 64
LANES = 128
X = 4
Y = 4
Z = 8
R = 4
ALL = (0, 1, 2, 3)
FIRST = ((2, ALL), (0, (0, 1)))
SECOND = ((3, ALL), (1, ALL), (0, (2, 3)))
PARTS = 4
ADD_FLOPS = 10**11
START_Z = 5


def vmem():
    return pl.BlockSpec(memory_space=pltpu.VMEM)


def hbm():
    return pl.BlockSpec(memory_space=pltpu.HBM)


def in_hbm(value):
    return pltpu.with_memory_space_constraint(value, pltpu.HBM)


def count(pieces):
    return sum(2 * Z * len(rs) for _, rs in pieces)


def here():
    me = lax.axis_index("pair")
    return lax.rem(me, X), lax.rem(lax.div(me, X), Y), lax.axis_index("blk")


def split(value):
    high = value.astype(jnp.bfloat16)
    low = (value - high.astype(jnp.float32)).astype(jnp.bfloat16)
    return high, low


def dot(a, b):
    return jnp.dot(a, b, preferred_element_type=jnp.float32)


def product(a_high, a_low, b_high, b_low):
    rows = a_high.shape[0]
    both = dot(jnp.concatenate([a_high, a_low], axis=0), b_high)
    return both[:rows] + (both[rows:] + dot(a_high, b_low))


def tile_rows(mask_ref, shift, width):
    tiles = mask_ref.shape[1]
    column = lax.div(lax.broadcasted_iota(jnp.int32, (tiles, width), 1), TILE)
    spread = lax.rem(column + shift, tiles) == lax.broadcasted_iota(jnp.int32, (tiles, width), 0)
    return dot(mask_ref[...].astype(jnp.float32), spread.astype(jnp.float32))


def first_kernel(t_ref, mask_ref, out_ref, held_ref, mask_held, sems):
    width = t_ref.shape[3]
    tiles = width // LANES
    x, y, blk = here()
    partner = x + 1 - 2 * lax.rem(x, 2)
    mask_copy = pltpu.make_async_copy(mask_ref.at[0], mask_held, sems.at[len(FIRST) * tiles])
    mask_copy.start()
    copies = []
    for t in range(tiles):
        lanes = pl.multiple_of(lax.rem(t + blk * (tiles // 2), tiles) * LANES, LANES)
        for n, (dy, _) in enumerate(FIRST):
            copy = pltpu.make_async_copy(
                t_ref.at[:, lax.rem(y + dy, Y), :, pl.ds(lanes, LANES)],
                held_ref.at[t, n],
                sems.at[t * len(FIRST) + n],
            )
            copy.start()
            copies.append(copy)
    mask_copy.wait()
    mask = tile_rows(mask_held, blk * (mask_ref.shape[2] // 2), width)
    for t in range(tiles):
        cols = pl.ds(t * LANES, LANES)
        m = mask[:, t * LANES : (t + 1) * LANES]
        at = 0
        for n, (_, rs) in enumerate(FIRST):
            copies[t * len(FIRST) + n].wait()
            rows = held_ref.at[t, n].reshape(Z * X * R, LANES)
            for r in rs:
                for h in range(2):
                    value = rows[pl.ds(end(partner, h) * R + r, Z, X * R), :]
                    out_ref[pl.ds(at, Z), cols] = value * m
                    at += Z


def end(x, h):
    outer = (x == 0) | (x == X - 1)
    return jnp.where(outer, h * (X - 1), 1 + h)


def near_kernel(
    t_ref, mask_ref, w_ref, after_ref, rest_ref, part_ref, high_ref, low_ref, held_ref, mask_held, w_held, sems, w_sems
):
    del after_ref
    rows, width = t_ref.shape[1:]
    x, y, blk = here()
    partner = x + 1 - 2 * lax.rem(x, 2)
    plane = X * Y * R
    tiles = width // LANES
    mask_copy = pltpu.make_async_copy(mask_ref.at[0], mask_held, sems.at[tiles])
    mask_copy.start()
    copies = []
    for t in range(tiles):
        copy = pltpu.make_async_copy(t_ref.at[0, :, pl.ds(t * LANES, LANES)], held_ref.at[t], sems.at[t])
        copy.start()
        copies.append(copy)
    w_copies = start_weights(w_ref, w_held, w_sems)
    mask_copy.wait()
    mask = tile_rows(mask_held, 0, width)
    wanted = [(piece, x) for piece in FIRST + SECOND] + [(piece, partner) for piece in SECOND]
    for t in range(tiles):
        copies[t].wait()
        cols = pl.ds(t * LANES, LANES)
        m = mask[:, t * LANES : (t + 1) * LANES]
        at = 0
        for (dy, rs), device in wanted:
            for r in rs:
                for h in range(2):
                    base = (lax.rem(y + dy, Y) * X + end(device, h)) * R
                    rest_ref[pl.ds(at, Z), cols] = held_ref[t, pl.ds(base + r, Z, plane), :] * m
                    at += Z
    contract(w_copies, blk, rest_ref, None, [part_ref], high_ref, low_ref, w_held)


def start_weights(w_ref, held_ref, sems):
    k = lax.rem(here()[0], 2)
    piece = w_ref.shape[1] // PARTS
    copies = []
    for which, of in enumerate((k, 1 - k)):
        for q in range(PARTS):
            copy = pltpu.make_async_copy(
                w_ref.at[of, pl.ds(q * piece, piece)],
                held_ref.at[which, pl.ds(q * piece, piece)],
                sems.at[which, q],
            )
            copy.start()
            copies.append(copy)
    return copies


def contract(copies, half, x_ref, first_ref, part_refs, high_ref, low_ref, held_ref):
    depth = held_ref.shape[1]
    x_high, x_low = split(x_ref[:, pl.ds(pl.multiple_of(half * depth, depth), depth)])
    for copy in copies[:PARTS]:
        copy.wait()
    total = product(x_high, x_low, *split(held_ref[0]))
    if first_ref is not None:
        total = first_ref[...] + total
    base = 0
    for part_ref in part_refs:
        size = part_ref.shape[0]
        part_ref[...] = total[base : base + size]
        base += size
    for copy in copies[PARTS:]:
        copy.wait()
    o_high, o_low = split(held_ref[1])
    high_ref[...] = o_high
    low_ref[...] = o_low


def far_kernel(x_ref, w_ref, first_ref, *refs):
    *part_refs, high_ref, low_ref, held_ref, sems = refs
    copies = start_weights(w_ref, held_ref, sems)
    contract(copies, 1 - here()[2], x_ref, first_ref, part_refs, high_ref, low_ref, held_ref)


def last_kernel(got_ref, high0_ref, low0_ref, high1_ref, low1_ref, part_ref, out_ref):
    depth = high0_ref.shape[0]
    total = part_ref[...]
    for n, (high_ref, low_ref) in enumerate(((high0_ref, low0_ref), (high1_ref, low1_ref))):
        total = total + product(*split(got_ref[:, n * depth : (n + 1) * depth]), high_ref[...], low_ref[...])
    put([out_ref], total, FIRST, True)


def put(out_refs, total, pieces, joined):
    tiles = total.shape[1] // LANES
    whole = sum(len(rs) for _, rs in pieces) * tiles
    row, start = 0, 0
    for n, (_, rs) in enumerate(pieces):
        out_ref = out_refs[0 if joined else n]
        block = whole if joined else len(rs) * tiles
        for j in range(len(rs)):
            for h in range(2):
                for t in range(tiles):
                    rows = pltpu.roll(total[row : row + Z, t * LANES : (t + 1) * LANES], Z - START_Z, 0)
                    out_ref[pl.ds(h * block + start + t * len(rs) + j, Z, 2 * block), :] = rows
                row += Z
        start += len(rs) * tiles if joined else 0


def sum_kernel(piece, got_ref, part_ref, out_ref):
    put([out_ref], got_ref[...] + part_ref[...], (piece,), False)


def turn_kernel(in_ref, *out_refs):
    whole, start = in_ref.shape[0] // (2 * Z), 0
    for out_ref in out_refs:
        block = out_ref.shape[0] // (2 * Z)
        for n in range(2 * Z):
            out_ref[pl.ds(n * block, block), :] = in_ref[pl.ds(n * whole + start, block), :]
        start += block


def gather_kernel(*refs):
    *in_refs, out_ref = refs
    whole, start = out_ref.shape[0] // (2 * Z), 0
    for in_ref in in_refs:
        block = in_ref.shape[0] // (2 * Z)
        for n in range(2 * Z):
            out_ref[pl.ds(n * whole + start, block), :] = in_ref[pl.ds(n * block, block), :]
        start += block


def merge_kernel(*refs):
    *moved_refs, second_ref, out_ref = refs
    block = out_ref.shape[0] // (2 * Y * Z)
    tiles = block // R
    whole = second_ref.shape[0] // (2 * Z)
    _, here_y, _ = here()
    sources = [(dy, rs, ref, len(rs) * tiles, 0) for (dy, rs), ref in zip(FIRST, moved_refs)]
    start = 0
    for dy, rs in SECOND:
        sources.append((dy, rs, second_ref, whole, start))
        start += len(rs) * tiles
    for dy, rs, ref, pitch, start in sources:
        y = lax.rem(here_y - dy + Y, Y)
        for n in range(2 * Z):
            z, h = (n // 2 + START_Z) % Z, n % 2
            to = pl.multiple_of(((z * Y + y) * 2 + h) * block, block)
            at = n * pitch + start
            if len(rs) == R:
                out_ref[pl.ds(to, block), :] = ref[pl.ds(at, block), :]
            else:
                for j, r in enumerate(rs):
                    out_ref[pl.ds(to + r, tiles, R), :] = ref[pl.ds(at + j, tiles, len(rs)), :]


def call(kernel, name, out_shape, in_specs, scratch=(), flops=1000):
    return pl.pallas_call(
        kernel,
        out_shape=out_shape,
        in_specs=in_specs,
        out_specs=jax.tree.map(lambda _: vmem(), out_shape),
        scratch_shapes=list(scratch),
        compiler_params=pltpu.CompilerParams(vmem_limit_bytes=24 * 2**20),
        cost_estimate=pl.CostEstimate(flops=flops, bytes_accessed=1000, transcendentals=0),
        name=name,
    )


def on_device(n_pair, groups, amplitudes, domain_mask, integrals):
    f32, bf16 = jnp.float32, jnp.bfloat16

    def of(*shape, dtype=f32):
        return jax.ShapeDtypeStruct(shape, dtype)

    rows, width = amplitudes.shape[1:]
    depth, columns = integrals.shape[1:]
    kept = rows // 2
    dests = kept // R
    tiles = columns // LANES
    swap = [(p, p ^ 1) for p in range(n_pair)]
    other = lax.ppermute(integrals, "blk", [(0, 1), (1, 0)])
    n_tiles = width // LANES
    n_rest = count(FIRST) + 2 * count(SECOND)
    mask_scratch = pltpu.VMEM(domain_mask.shape[1:], jnp.int32)
    send0 = call(
        first_kernel,
        "first",
        of(count(FIRST), width),
        [hbm(), hbm()],
        [
            pltpu.VMEM((n_tiles, len(FIRST), Z, X * R, LANES), f32),
            mask_scratch,
            pltpu.SemaphoreType.DMA((len(FIRST) * n_tiles + 1,)),
        ],
    )(in_hbm(amplitudes.reshape(Z, Y, X * R, width)), in_hbm(domain_mask))
    got0 = lax.ppermute(send0, "pair", swap)
    halves_w = [of(depth, columns, dtype=bf16)] * 2
    scratch = [pltpu.VMEM((2, depth, columns), f32), pltpu.SemaphoreType.DMA((2, PARTS))]
    rest, part, high0, low0 = call(
        near_kernel,
        "near",
        [of(n_rest, width), of(n_rest, columns)] + halves_w,
        [hbm(), hbm(), hbm(), pl.BlockSpec(memory_space=pl.ANY)],
        [pltpu.VMEM((n_tiles, rows, LANES), f32), mask_scratch, scratch[0], pltpu.SemaphoreType.DMA((n_tiles + 1,)), scratch[1]],
    )(in_hbm(amplitudes), in_hbm(domain_mask), in_hbm(integrals), send0)
    sizes = [count((piece,)) for piece in SECOND]
    part0, *parts, high1, low1 = call(
        far_kernel,
        "far",
        [of(n, columns) for n in [count(FIRST)] + sizes + sizes] + halves_w,
        [vmem(), hbm(), vmem()],
        scratch,
    )(rest, other, part)
    parts, sends = parts[: len(SECOND)], parts[len(SECOND) :]
    got = [lax.ppermute(send, "pair", swap) for send in sends]

    def along_y(value, dy):
        perm = []
        for p in range(n_pair):
            pz, py, px = p // (X * Y), p // X % Y, p % X
            perm.append((p, (pz * Y + (py + dy) % Y) * X + px))
        return lax.ppermute(value, "pair", perm)

    def across(block):
        out = lax.all_to_all(
            block.reshape(2 * Z, -1, LANES),
            "pair",
            split_axis=0,
            concat_axis=0,
            tiled=True,
            axis_index_groups=groups,
        )
        return out.reshape(-1, LANES)


    def blocks(pieces):
        return [of(count((piece,)) * tiles, LANES) for piece in pieces]

    block0 = call(last_kernel, "last", of(count(FIRST) * tiles, LANES), [vmem()] * 6)(
        got0, high0, low0, high1, low1, part0
    )
    back0 = across(block0)
    pieces = []
    for n, (dy, rs) in enumerate(SECOND):
        value = call(
            functools.partial(sum_kernel, (dy, rs)),
            "sum",
            of(sizes[n] * tiles, LANES),
            [vmem()] * 2,
            (),
            1000 if dy else ADD_FLOPS,
        )(got[n], parts[n])
        pieces.append(along_y(value, dy) if dy else value)
    block1 = call(gather_kernel, "gather", of(count(SECOND) * tiles, LANES), [vmem()] * len(pieces))(*pieces)
    back1 = across(block1)
    moved = call(turn_kernel, "turn", blocks(FIRST), [vmem()])(back0) if len(FIRST) > 1 else [back0]
    moved = [along_y(value, dy) if dy else value for value, (dy, _) in zip(moved, FIRST)]
    whole = call(merge_kernel, "merge", of(dests * R * tiles, LANES), [vmem()] * (len(moved) + 1))(*moved, back1)
    return whole.reshape(dests, tiles, R, LANES).transpose(0, 2, 1, 3).reshape(dests, R, columns)


def solution(mesh):
    n_pair = mesh.shape["pair"]
    groups = [
        [((z + START_Z) % Z * Y + y) * X + x for z in range(Z) for x in pair] for y in range(Y) for pair in ((0, 3), (1, 2))
    ]
    return jax.shard_map(
        functools.partial(on_device, n_pair, groups),
        mesh=mesh,
        in_specs=(P("pair", "blk", None), P("pair", "blk", None), P(None, "blk", None)),
        out_specs=P(None, ("blk", "pair"), None),
        check_vma=False,
    )
```
